32 devices in a mesh: clip: 8 (over z, x), seq: 4 (over y, core).
Axes of the slice: x: 2, y: 2, z: 4, core: 2. Of those that a mesh axis runs over, the one named last changes fastest.
Arguments:
- frames: bfloat16 [8, 1024, 768], P('clip', 'seq'), may hold values from -6 to 6
- out_grad: bfloat16 [8, 1024, 768], P('clip', 'seq'), may hold values from -6 to 6
- attn_in: bfloat16 [2, 768, 2304], P(None, ('clip', 'seq')), may hold values from -0.21875 to 0.21875
- attn_out: bfloat16 [2, 768, 768], P(None, ('clip', 'seq')), may hold values from -3.5 to 3.5
- mlp_in: bfloat16 [2, 768, 3072], P(None, ('clip', 'seq')), may hold values from -0.21875 to 0.21875
- mlp_out: bfloat16 [2, 3072, 768], P(None, ('clip', 'seq')), may hold values from -0.109375 to 0.109375
- norm_gains: bfloat16 [2, 2, 768], P(None, None, ('clip', 'seq')), may hold values from 0.25 to 1.75
- shifts: bfloat16 [2, 6, 768], P(None, None, ('clip', 'seq')), may hold values from -3 to 3
- mlp_bias: bfloat16 [2, 3072], P(None, ('clip', 'seq')), may hold values from -3 to 3
Outputs:
- encoded: bfloat16 [8, 1024, 768], P('clip', 'seq')
- frames_grad: float32 [8, 1024, 768], P('clip', 'seq')
- attn_in_grad: float32 [2, 768, 2304], P(None, ('clip', 'seq'))
- attn_out_grad: float32 [2, 768, 768], P(None, ('clip', 'seq'))
- mlp_in_grad: float32 [2, 768, 3072], P(None, ('clip', 'seq'))
- mlp_out_grad: float32 [2, 3072, 768], P(None, ('clip', 'seq'))
- norm_gains_grad: float32 [2, 2, 768], P(None, None, ('clip', 'seq'))
- shifts_grad: float32 [2, 6, 768], P(None, None, ('clip', 'seq'))
- mlp_bias_grad: float32 [2, 3072], P(None, ('clip', 'seq'))
The draws below stay inside these ranges and needn't reach their ends.
All inputs are finite; a program needn't handle non-finite values.
Results may differ from the reference program's by a relative error of at most 0.015.
Values may be sent and summed in bfloat16 or wider, within the bound.
A program may use at most 192 MiB of HBM per device.

```python
import jax
import jax.numpy as jnp
from jax import lax

D = 768
H = 12
HD = 64
FF = 3072
LAYERS = 2
FR_DEV = 256
LENGTH = 1024
CLIPS = 8
TOKENS = 8192
N_SEQ = 4


def steps_of(key, shape, pieces, least, high):
    loudness, own = 1.0, jax.random.fold_in(key, 6)
    for position, shards_of in pieces:
        steps = jnp.exp(jax.random.uniform(jax.random.fold_in(own, position), (shards_of,), jnp.float32, least / len(pieces), high / len(pieces)))
        loudness = loudness * jnp.repeat(steps, shape[position] // shards_of).reshape([-1 if axis == position else 1 for axis in range(len(shape))])
    return loudness


def centred(own_key, shape, deviation, bound, cuts=(), dtype=jnp.bfloat16):
    drawn = deviation * jax.random.normal(own_key, shape, jnp.float32)
    if cuts:
        drawn = drawn * steps_of(own_key, shape, cuts, -0.22, 0.18)
    return jnp.clip(drawn, -bound, bound).astype(dtype)


def setup_inputs(seed: int = 0) -> dict:
    streams_of = jax.random.split(jax.random.key(seed), 10)
    return {
        "frames": centred(streams_of[0], (CLIPS, LENGTH, D), 1.0, 6.0, ((0, 8), (1, 4))),
        "out_grad": centred(streams_of[1], (CLIPS, LENGTH, D), 1.0, 6.0, ((0, 8), (1, 4))),
        "attn_in": centred(streams_of[2], (LAYERS, D, 3 * D), D ** -0.5, 0.21875, ((1, 32),)),
        "attn_out": centred(streams_of[3], (LAYERS, D, D), (max(1, 4 * D // (FR_DEV * N_SEQ))) ** -0.5, 3.5, ((1, 32),)),
        "mlp_in": centred(streams_of[4], (LAYERS, D, FF), D ** -0.5, 0.21875, ((1, 32),)),
        "mlp_out": centred(streams_of[5], (LAYERS, FF, D), FF ** -0.5, 0.109375, ((1, 32),)),
        "norm_gains": jnp.clip(1.0 + 0.15 * jax.random.normal(streams_of[6], (LAYERS, 2, D), jnp.float32), 0.25, 1.75).astype(jnp.bfloat16),
        "shifts": centred(streams_of[7], (LAYERS, 6, D), 0.5, 3.0, ((2, 32),)),
        "mlp_bias": centred(streams_of[8], (LAYERS, FF), 0.5, 3.0, ((1, 32),)),
    }


@jax.custom_vjp
def low(v):
    return lax.optimization_barrier(v.astype(jnp.bfloat16)).astype(jnp.float32)

@jax.custom_vjp
def low_back(v):
    return v

def low_keep(v):
    return (low(v), None)

def low_pass(kept, grad):
    return (grad,)

def back_keep(v):
    return (v, None)

def back_low(kept, grad):
    return (low(grad),)
low.defvjp(low_keep, low_pass)
low_back.defvjp(back_keep, back_low)
eps_norm = 1e-05

def matmul(left, right):
    return jnp.dot(left, right, precision=lax.Precision.HIGHEST, preferred_element_type=jnp.float32)

def normalize(rows, gain, shift):
    center = rows - lax.optimization_barrier(jnp.mean(rows, axis=-1, keepdims=True))
    variance = lax.optimization_barrier(jnp.mean(center * center, axis=-1, keepdims=True))
    return center * lax.rsqrt(variance + eps_norm) * gain + shift

def to_heads(rows):
    return rows.reshape(rows.shape[0], H, HD).transpose(1, 0, 2)

def from_heads(heads):
    return heads.transpose(1, 0, 2).reshape(heads.shape[1], H * HD)

def head_attend(operands):
    queries, all_keys, all_values = operands
    score_scale = HD ** (-0.5)
    scores = low_back(matmul(queries, all_keys.T) * score_scale)
    attn_probs = jax.nn.softmax(scores, axis=-1)
    return matmul(low(attn_probs), all_values)

def clip_attend(operands):
    queries, all_keys, all_values = operands
    heads = lax.map(jax.checkpoint(head_attend), (to_heads(queries), to_heads(all_keys), to_heads(all_values)))
    return from_heads(heads)

def encoder_layer(residual, attn_in, attn_out, mlp_in, mlp_out, norm_gains, shifts, mlp_bias):
    normed = low(normalize(residual, norm_gains[0], shifts[0]))
    qkv_bias = jnp.concatenate([shifts[1], jnp.zeros_like(shifts[1]), shifts[2]])
    projected = low_back(low(matmul(normed, attn_in) + qkv_bias))
    queries = projected[:, :D].reshape(CLIPS, LENGTH, D)
    all_keys = projected[:, D:2 * D].reshape(CLIPS, LENGTH, D)
    all_values = projected[:, 2 * D:].reshape(CLIPS, LENGTH, D)
    attended = lax.map(clip_attend, (queries, all_keys, all_values)).reshape(TOKENS, D)
    attended = low_back(low(attended))
    middle = residual + low_back(matmul(attended, attn_out) + shifts[3])
    normed_two = low(normalize(middle, norm_gains[1], shifts[4]))
    pre_gelu = low_back(matmul(normed_two, mlp_in) + mlp_bias)
    hidden = low(jax.nn.gelu(pre_gelu, approximate=False))
    return middle + low_back(matmul(hidden, mlp_out) + shifts[5])

def reference(frames, out_grad, attn_in, attn_out, mlp_in, mlp_out, norm_gains, shifts, mlp_bias):
    params = tuple((tensor.astype(jnp.float32) for tensor in (attn_in, attn_out, mlp_in, mlp_out, norm_gains, shifts, mlp_bias)))

    def forward(residual, weights):
        for layer_index in range(LAYERS):
            residual = encoder_layer(residual, *[tensor[layer_index] for tensor in weights])
        return residual
    flat_frames = frames.astype(jnp.float32).reshape(TOKENS, D)
    encoded, pullback = jax.vjp(forward, flat_frames, params)
    frames_grad, gradients = pullback(out_grad.astype(jnp.float32).reshape(TOKENS, D))
    encoded = encoded.astype(jnp.bfloat16).reshape(CLIPS, LENGTH, D)
    frames_grad = frames_grad.reshape(CLIPS, LENGTH, D)
    return (encoded, frames_grad, gradients[0], gradients[1], gradients[2], gradients[3], gradients[4], gradients[5], gradients[6])
```

```python
import functools

import jax
import jax.numpy as jnp
from jax import lax
from jax.experimental import pallas as pl
from jax.experimental.pallas import tpu as pltpu
from jax.sharding import PartitionSpec as P

D = 768
H = 12
HD = 64


eps_norm = 1e-05
root_half = 0.7071067811865476
inv_root_two_pi = 0.3989422804014327


def product(left, right):
    return jnp.dot(left, right, preferred_element_type=jnp.float32)


def product_left(left, right):
    return lax.dot_general(
        left, right, (((0,), (0,)), ((), ())), preferred_element_type=jnp.float32
    )


def product_right(left, right):
    return lax.dot_general(
        left, right, (((1,), (1,)), ((), ())), preferred_element_type=jnp.float32
    )


def norm_forward(rows, gain, shift):
    center = rows - jnp.mean(rows, axis=1, keepdims=True)
    inv_scale = lax.rsqrt(jnp.mean(center * center, axis=1, keepdims=True) + eps_norm)
    unit_rows = center * inv_scale
    return (unit_rows * gain + shift, unit_rows, inv_scale)


def norm_backward(upstream, unit_rows, inv_scale, gain):
    scaled = upstream * gain
    mean_plain = jnp.mean(scaled, axis=1, keepdims=True)
    mean_unit = jnp.mean(scaled * unit_rows, axis=1, keepdims=True)
    back = inv_scale * (scaled - mean_plain - unit_rows * mean_unit)
    return (back, jnp.sum(upstream * unit_rows, axis=0), jnp.sum(upstream, axis=0))


def gelu_slope(pre_gelu):
    cumulative = 0.5 * (1.0 + lax.erf(pre_gelu * root_half))
    density = jnp.exp(-0.5 * pre_gelu * pre_gelu) * inv_root_two_pi
    return cumulative + pre_gelu * density


def column_sums(rows):
    return jnp.sum(rows.astype(jnp.float32), axis=0)


def bit_of(index, weight):
    return lax.rem(lax.div(index, weight), 2)


def flip(index, weight):
    return index + weight - 2 * weight * bit_of(index, weight)


def bit_orders(clip_size, seq_size, with_clip=True):
    high = []
    weight = clip_size * seq_size // 2
    while weight >= seq_size and with_clip:
        high.append(weight)
        weight //= 2
    low = []
    weight = seq_size // 2
    while weight >= 1:
        low.append(weight)
        weight //= 2
    first = high + low
    if not high:
        return (first, first)
    second = high[:-1] + [low[0], high[-1]] + low[1:]
    return (first, second)


def spread(position, weights):
    total = 0
    for place, weight in enumerate(weights):
        total = total + weight * lax.rem(lax.div(position, 2**place), 2)
    return total


def partner_id(weight, seq_size):
    clip_at, seq_at = lax.axis_index("clip"), lax.axis_index("seq")
    if weight < seq_size:
        return {"clip": clip_at, "seq": flip(seq_at, weight)}
    return {"clip": flip(clip_at, weight // seq_size), "seq": seq_at}


def greet(weights, seq_size):
    barrier = pltpu.get_barrier_semaphore()
    for weight in weights:
        pl.semaphore_signal(
            barrier,
            inc=1,
            device_id=partner_id(weight, seq_size),
            device_id_type=pl.DeviceIdType.MESH,
        )
    pl.semaphore_wait(barrier, len(weights))


def round_up(value, step):
    return (value + step - 1) // step * step


def halves_of(rows):
    first = round_up(rows // 2, 16)
    if first >= rows:
        return ((0, rows),)
    return ((0, first), (first, rows - first))


def cube_gather(shard, clip_size, seq_size, with_clip, collective_id):
    parts, rows, columns = shard.shape
    count = clip_size * seq_size if with_clip else seq_size
    orders = bit_orders(clip_size, seq_size, with_clip)
    chains = [
        (part, start, size, orders[place % 2])
        for part in range(parts)
        for place, (start, size) in enumerate(halves_of(rows))
    ]
    stages = len(orders[0])

    def kernel(in_ref, out_ref, own_sem, send_sem, recv_sem):
        greet(orders[0], seq_size)
        me = lax.axis_index("seq")
        if with_clip:
            me = lax.axis_index("clip") * seq_size + me
        own = []
        for part in range(parts):
            copy = pltpu.make_async_copy(in_ref.at[part], out_ref.at[part, me], own_sem.at[part])
            copy.start()
            own.append(copy)
        for copy in own:
            copy.wait()

        def start_stage(chain_at, stage):
            part, start, size, order = chains[chain_at]
            weight = order[stage]
            base = me
            for done in order[:stage]:
                base = base - done * bit_of(me, done)

            def one(position, carry):
                place = base + spread(position, order[:stage])
                block = out_ref.at[part, place, pl.ds(start, size)]
                pltpu.make_async_remote_copy(
                    src_ref=block,
                    dst_ref=block,
                    send_sem=send_sem.at[chain_at, stage],
                    recv_sem=recv_sem.at[chain_at, stage],
                    device_id=partner_id(weight, seq_size),
                    device_id_type=pl.DeviceIdType.MESH,
                ).start()
                return carry

            if stage == 0:
                one(0, 0)
            else:
                lax.fori_loop(0, 2**stage, one, 0)

        def wait_stage(chain_at, stage):
            part, start, size, order = chains[chain_at]
            block = out_ref.at[part, pl.ds(0, 2**stage), pl.ds(start, size)]
            pltpu.make_async_remote_copy(
                src_ref=block,
                dst_ref=block,
                send_sem=send_sem.at[chain_at, stage],
                recv_sem=recv_sem.at[chain_at, stage],
                device_id=partner_id(order[stage], seq_size),
                device_id_type=pl.DeviceIdType.MESH,
            ).wait()

        for tick in range(stages + parts):
            for chain_at, chain in enumerate(chains):
                stage = tick - chain[0]
                if 1 <= stage <= stages:
                    wait_stage(chain_at, stage - 1)
                if 0 <= stage < stages:
                    start_stage(chain_at, stage)

    return pl.pallas_call(
        kernel,
        out_shape=jax.ShapeDtypeStruct((parts, count, rows, columns), shard.dtype),
        in_specs=[pl.BlockSpec(memory_space=pl.ANY)],
        out_specs=pl.BlockSpec(memory_space=pl.ANY),
        scratch_shapes=[
            pltpu.SemaphoreType.DMA((parts,)),
            pltpu.SemaphoreType.DMA((len(chains), stages)),
            pltpu.SemaphoreType.DMA((len(chains), stages)),
        ],
        compiler_params=pltpu.CompilerParams(
            collective_id=collective_id, has_side_effects=True, vmem_limit_bytes=16 * 2**20
        ),
    )(shard)


def cube_scatter(terms, clip_size, seq_size, with_clip, collective_id, out_dtype=jnp.float32):
    count, rows, columns = terms.shape
    orders = [order[::-1] for order in bit_orders(clip_size, seq_size, with_clip)]
    chains = [
        (start, size, orders[place % 2]) for place, (start, size) in enumerate(halves_of(rows))
    ]
    stages = len(orders[0])
    offsets = [sum(count // 2 ** (s + 1) for s in range(stage)) for stage in range(stages)]

    def kernel(in_ref, out_ref, total, landed, own_sem, send_sem, recv_sem):
        greet(orders[0], seq_size)
        me = lax.axis_index("seq")
        if with_clip:
            me = lax.axis_index("clip") * seq_size + me

        def places(chain_at, stage):
            order = chains[chain_at][2]
            base = me
            for later in order[stage:]:
                base = base - later * bit_of(me, later)
            weight = order[stage]
            mine = base + weight * bit_of(me, weight)
            theirs = base + weight - weight * bit_of(me, weight)
            return mine, theirs, order[stage + 1 :], weight

        def start_stage(chain_at, stage):
            start, size, order = chains[chain_at]
            mine, theirs, rest, weight = places(chain_at, stage)
            source = in_ref if stage == 0 else total

            def one(position, carry):
                pltpu.make_async_remote_copy(
                    src_ref=source.at[theirs + spread(position, rest), pl.ds(start, size)],
                    dst_ref=landed.at[offsets[stage] + position, pl.ds(start, size)],
                    send_sem=send_sem.at[chain_at, stage],
                    recv_sem=recv_sem.at[chain_at, stage],
                    device_id=partner_id(weight, seq_size),
                    device_id_type=pl.DeviceIdType.MESH,
                ).start()
                return carry

            if stage == stages - 1:
                one(0, 0)
            else:
                lax.fori_loop(0, 2 ** (stages - 1 - stage), one, 0)

        def load_own(chain_at):
            start, size, order = chains[chain_at]
            mine, theirs, rest, weight = places(chain_at, 0)

            def one(position, carry):
                place = mine + spread(position, rest)
                pltpu.make_async_copy(
                    in_ref.at[place, pl.ds(start, size)],
                    total.at[place, pl.ds(start, size)],
                    own_sem.at[chain_at],
                ).start()
                return carry

            lax.fori_loop(0, count // 2, one, 0)

        def wait_own(chain_at):
            start, size, order = chains[chain_at]
            block = pl.ds(0, count // 2), pl.ds(start, size)
            pltpu.make_async_copy(in_ref.at[block], total.at[block], own_sem.at[chain_at]).wait()

        def finish_stage(chain_at, stage):
            start, size, order = chains[chain_at]
            mine, theirs, rest, weight = places(chain_at, stage)
            blocks = 2 ** (stages - 1 - stage)
            source = in_ref if stage == 0 else total
            pltpu.make_async_remote_copy(
                src_ref=source.at[pl.ds(0, blocks), pl.ds(start, size)],
                dst_ref=landed.at[pl.ds(offsets[stage], blocks), pl.ds(start, size)],
                send_sem=send_sem.at[chain_at, stage],
                recv_sem=recv_sem.at[chain_at, stage],
                device_id=partner_id(weight, seq_size),
                device_id_type=pl.DeviceIdType.MESH,
            ).wait()
            if stage == 0:
                wait_own(chain_at)
            tiles = size // 16

            def add(step, carry):
                position, tile = lax.div(step, tiles), lax.rem(step, tiles)
                place = mine + spread(position, rest)
                row = pl.ds(pl.multiple_of(start + tile * 16, 16), 16)
                summed = total[place, row, :].astype(jnp.float32) + landed[
                    offsets[stage] + position, row, :
                ].astype(jnp.float32)
                if stage == stages - 1:
                    out_ref[row, :] = summed.astype(out_ref.dtype)
                else:
                    total[place, row, :] = summed.astype(jnp.bfloat16)
                return carry

            lax.fori_loop(0, blocks * tiles, add, 0)

        for chain_at in range(len(chains)):
            start_stage(chain_at, 0)
        for chain_at in range(len(chains)):
            load_own(chain_at)
        for stage in range(stages):
            for chain_at in range(len(chains)):
                finish_stage(chain_at, stage)
                if stage + 1 < stages:
                    start_stage(chain_at, stage + 1)

    return pl.pallas_call(
        kernel,
        out_shape=jax.ShapeDtypeStruct((rows, columns), out_dtype),
        in_specs=[pl.BlockSpec(memory_space=pl.ANY)],
        out_specs=pl.BlockSpec(memory_space=pltpu.VMEM),
        scratch_shapes=[
            pltpu.VMEM((count, rows, columns), terms.dtype),
            pltpu.VMEM((count - 1, rows, columns), terms.dtype),
            pltpu.SemaphoreType.DMA((len(chains),)),
            pltpu.SemaphoreType.DMA((len(chains), stages)),
            pltpu.SemaphoreType.DMA((len(chains), stages)),
        ],
        compiler_params=pltpu.CompilerParams(
            collective_id=collective_id, has_side_effects=True, vmem_limit_bytes=48 * 2**20
        ),
    )(terms)


def head_pair(ref, head):
    return ref[:, head * HD : (head + 1) * HD]


def probabilities(query, key):
    scores = product_right(query, key) * (HD ** (-0.5))
    powers = jnp.exp(scores - jnp.max(scores, axis=1, keepdims=True))
    return powers * (1.0 / jnp.sum(powers, axis=1, keepdims=True))


def attend_forward_kernel(q_ref, k_ref, v_ref, o_ref):
    outputs = []
    for head in range(2):
        probs = probabilities(head_pair(q_ref, head), head_pair(k_ref, head))
        outputs.append(product(probs.astype(jnp.bfloat16), head_pair(v_ref, head)))
    o_ref[...] = jnp.concatenate(outputs, axis=1).astype(o_ref.dtype)


def attend_backward_kernel(q_ref, k_ref, v_ref, go_ref, gq_ref, gk_ref, gv_ref):
    grads = ([], [], [])
    for head in range(2):
        query, key = head_pair(q_ref, head), head_pair(k_ref, head)
        value, upstream = head_pair(v_ref, head), head_pair(go_ref, head)
        probs = probabilities(query, key)
        grad_probs = product_right(upstream, value)
        inner = jnp.sum(grad_probs * probs, axis=1, keepdims=True)
        grad_scores = (probs * (grad_probs - inner)).astype(jnp.bfloat16)
        grads[0].append(product(grad_scores, key) * (HD ** (-0.5)))
        grads[1].append(product_left(grad_scores, query) * (HD ** (-0.5)))
        grads[2].append(product_left(probs.astype(jnp.bfloat16), upstream))
    for ref, pieces in zip((gq_ref, gk_ref, gv_ref), grads):
        ref[...] = jnp.concatenate(pieces, axis=1).astype(ref.dtype)


def attend_forward(projected, key_values):
    rows, length = projected.shape[0], key_values.shape[0]
    pairs = D // (2 * HD)
    return pl.pallas_call(
        attend_forward_kernel,
        grid=(pairs,),
        out_shape=jax.ShapeDtypeStruct((rows, D), jnp.bfloat16),
        in_specs=[
            pl.BlockSpec((rows, 2 * HD), lambda pair: (0, pair)),
            pl.BlockSpec((length, 2 * HD), lambda pair: (0, pair)),
            pl.BlockSpec((length, 2 * HD), lambda pair: (0, pair + pairs)),
        ],
        out_specs=pl.BlockSpec((rows, 2 * HD), lambda pair: (0, pair)),
        compiler_params=pltpu.CompilerParams(vmem_limit_bytes=40 * 2**20),
    )(projected, key_values, key_values)


def attend_backward(projected, key_values, grad_attended):
    rows, length = projected.shape[0], key_values.shape[0]
    pairs = D // (2 * HD)
    return pl.pallas_call(
        attend_backward_kernel,
        grid=(pairs,),
        out_shape=(
            jax.ShapeDtypeStruct((rows, D), jnp.bfloat16),
            jax.ShapeDtypeStruct((length, D), jnp.bfloat16),
            jax.ShapeDtypeStruct((length, D), jnp.bfloat16),
        ),
        in_specs=[
            pl.BlockSpec((rows, 2 * HD), lambda pair: (0, pair)),
            pl.BlockSpec((length, 2 * HD), lambda pair: (0, pair)),
            pl.BlockSpec((length, 2 * HD), lambda pair: (0, pair + pairs)),
            pl.BlockSpec((rows, 2 * HD), lambda pair: (0, pair)),
        ],
        out_specs=(
            pl.BlockSpec((rows, 2 * HD), lambda pair: (0, pair)),
            pl.BlockSpec((length, 2 * HD), lambda pair: (0, pair)),
            pl.BlockSpec((length, 2 * HD), lambda pair: (0, pair)),
        ),
        compiler_params=pltpu.CompilerParams(vmem_limit_bytes=48 * 2**20),
    )(projected, key_values, key_values, grad_attended)


def pack_shards(attn_in, attn_out, mlp_in, mlp_out, norm_gains, shifts, mlp_bias):
    layers, depth = attn_in.shape[0], attn_in.shape[1]
    small = jnp.concatenate(
        [norm_gains.reshape(layers, -1), shifts.reshape(layers, -1), mlp_bias], axis=1
    )
    small_rows = (small.shape[1] + D - 1) // D
    small = jnp.pad(small, ((0, 0), (0, small_rows * D - small.shape[1])))
    small = small.reshape(layers, small_rows, D)
    blocks = [attn_in[:, :, at : at + D] for at in range(0, attn_in.shape[2], D)]
    blocks.append(attn_out)
    blocks += [mlp_in[:, :, at : at + D] for at in range(0, mlp_in.shape[2], D)]
    blocks += [mlp_out, small]
    rows = sum(block.shape[1] for block in blocks)
    padding = round_up(rows, 16) - rows
    blocks.append(jnp.zeros((layers, padding, D), attn_in.dtype))
    return jnp.concatenate(blocks, axis=1)


def columns_back(gathered, first, blocks, depth):
    count = gathered.shape[0]
    piece = gathered[:, first : first + blocks * depth].reshape(count, blocks, depth, D)
    return piece.transpose(0, 2, 1, 3).reshape(count * depth, blocks * D)


def unpack_layer(gathered, depth):
    count = gathered.shape[0]
    w_attn_in = columns_back(gathered, 0, 3, depth)
    w_attn_out = columns_back(gathered, 3 * depth, 1, depth)
    w_mlp_in = columns_back(gathered, 4 * depth, 4, depth)
    w_mlp_out = gathered[:, 8 * depth : 12 * depth].reshape(4 * count * depth, D)
    small_rows = (12 * depth + D - 1) // D
    small = gathered[:, 12 * depth : 12 * depth + small_rows].reshape(count, -1)
    small = small.astype(jnp.float32)
    gains = small[:, : 2 * depth].reshape(count, 2, depth).transpose(1, 0, 2).reshape(2, D)
    shift_rows = small[:, 2 * depth : 8 * depth].reshape(count, 6, depth)
    shift_rows = shift_rows.transpose(1, 0, 2).reshape(6, D)
    bias_mlp = small[:, 8 * depth : 12 * depth].reshape(4 * D)
    return (w_attn_in, w_attn_out, w_mlp_in, w_mlp_out, gains, shift_rows, bias_mlp)


def columns_apart(term, count):
    depth, blocks = term.shape[0] // count, term.shape[1] // D
    term = term.astype(jnp.bfloat16).reshape(count, depth, blocks, D)
    return term.transpose(0, 2, 1, 3).reshape(count, blocks * depth, D)


def pack_grads(grad_terms, count, rows):
    grad_attn_in, grad_attn_out, grad_mlp_in, grad_mlp_out, gains, shift_rows, bias = grad_terms
    depth = D // count
    small = jnp.concatenate(
        [
            gains.reshape(2, count, depth).transpose(1, 0, 2).reshape(count, -1),
            shift_rows.reshape(6, count, depth).transpose(1, 0, 2).reshape(count, -1),
            bias.reshape(count, -1),
        ],
        axis=1,
    ).astype(jnp.bfloat16)
    small_rows = (small.shape[1] + D - 1) // D
    small = jnp.pad(small, ((0, 0), (0, small_rows * D - small.shape[1])))
    blocks = [
        columns_apart(grad_attn_in, count),
        columns_apart(grad_attn_out, count),
        columns_apart(grad_mlp_in, count),
        grad_mlp_out.astype(jnp.bfloat16).reshape(count, 4 * depth, D),
        small.reshape(count, small_rows, D),
    ]
    padding = rows - sum(block.shape[1] for block in blocks)
    blocks.append(jnp.zeros((count, padding, D), jnp.bfloat16))
    return jnp.concatenate(blocks, axis=1)


def unpack_shard(summed, depth):
    def across(first, blocks):
        return jnp.concatenate(
            [summed[first + at * depth : first + (at + 1) * depth] for at in range(blocks)], axis=1
        )

    small_rows = (12 * depth + D - 1) // D
    small = summed[12 * depth : 12 * depth + small_rows].reshape(-1)
    return (
        across(0, 3),
        across(3 * depth, 1),
        across(4 * depth, 4),
        summed[8 * depth : 12 * depth],
        small[: 2 * depth].reshape(2, depth),
        small[2 * depth : 8 * depth].reshape(6, depth),
        small[8 * depth : 12 * depth],
    )


def layer_forward(residual, weights, sizes, layer_index):
    w_attn_in, w_attn_out, w_mlp_in, w_mlp_out, gain_rows, shift_rows, bias_mlp = weights
    normed = norm_forward(residual, gain_rows[0], shift_rows[0])[0].astype(jnp.bfloat16)
    qkv_bias = jnp.concatenate([shift_rows[1], jnp.zeros_like(shift_rows[1]), shift_rows[2]])
    projected = (product(normed, w_attn_in) + qkv_bias).astype(jnp.bfloat16)
    key_values = cube_gather(projected[None, :, D:], *sizes, False, 2 + layer_index)
    key_values = key_values.reshape(-1, 2 * D)
    attended = attend_forward(projected, key_values)
    middle = residual + product(attended, w_attn_out) + shift_rows[3]
    normed_two = norm_forward(middle, gain_rows[1], shift_rows[4])[0].astype(jnp.bfloat16)
    pre_gelu = product(normed_two, w_mlp_in) + bias_mlp
    hidden = jax.nn.gelu(pre_gelu, approximate=False).astype(jnp.bfloat16)
    result = middle + product(hidden, w_mlp_out) + shift_rows[5]
    saved = (residual, normed, projected, key_values, attended, middle, normed_two, pre_gelu, hidden)
    return (result, saved)


def layer_backward(upstream, saved, weights, sizes, layer_index):
    w_attn_in, w_attn_out, w_mlp_in, w_mlp_out, gain_rows, shift_rows, bias_mlp = weights
    residual, normed, projected, key_values, attended, middle, normed_two, pre_gelu, hidden = saved
    upstream_low = upstream.astype(jnp.bfloat16)
    grad_mlp_out = product_left(hidden, upstream_low)
    grad_bias_two = column_sums(upstream_low)
    grad_pre = (product_right(upstream_low, w_mlp_out) * gelu_slope(pre_gelu)).astype(jnp.bfloat16)
    grad_mlp_in = product_left(normed_two, grad_pre)
    grad_mlp_bias = column_sums(grad_pre)
    grad_normed_two = product_right(grad_pre, w_mlp_in)
    unit_two, scale_two = norm_forward(middle, gain_rows[1], shift_rows[4])[1:]
    back_two, grad_gain_two, grad_shift_two = norm_backward(
        grad_normed_two, unit_two, scale_two, gain_rows[1]
    )
    grad_middle = upstream + back_two
    middle_low = grad_middle.astype(jnp.bfloat16)
    grad_attn_out = product_left(attended, middle_low)
    grad_bias_out = column_sums(middle_low)
    grad_attended = product_right(middle_low, w_attn_out).astype(jnp.bfloat16)
    grad_queries, key_terms, value_terms = attend_backward(projected, key_values, grad_attended)
    rows = grad_queries.shape[0]
    terms = jnp.concatenate([key_terms, value_terms], axis=1).reshape(-1, rows, 2 * D)
    grad_key_values = cube_scatter(terms, *sizes, False, 4 + layer_index, jnp.bfloat16)
    grad_projected = jnp.concatenate([grad_queries, grad_key_values], axis=1)
    grad_attn_in = product_left(normed, grad_projected)
    projected_sums = column_sums(grad_projected)
    grad_normed = product_right(grad_projected, w_attn_in)
    unit_one, scale_one = norm_forward(residual, gain_rows[0], shift_rows[0])[1:]
    back_one, grad_gain_one, grad_shift_one = norm_backward(
        grad_normed, unit_one, scale_one, gain_rows[0]
    )
    grad_residual = grad_middle + back_one
    grad_gains = jnp.stack([grad_gain_one, grad_gain_two])
    grad_shifts = jnp.stack(
        [
            grad_shift_one,
            projected_sums[:D],
            projected_sums[2 * D :],
            grad_bias_out,
            grad_shift_two,
            grad_bias_two,
        ]
    )
    grad_terms = (
        grad_attn_in,
        grad_attn_out,
        grad_mlp_in,
        grad_mlp_out,
        grad_gains,
        grad_shifts,
        grad_mlp_bias,
    )
    return (grad_residual, grad_terms)


def body(sizes, frames, out_grad, *params):
    layers, depth = params[0].shape[0], params[0].shape[1]
    count = sizes[0] * sizes[1]
    groups, frame_count, width = frames.shape
    residual = frames.astype(jnp.float32).reshape(groups * frame_count, width)
    packed = pack_shards(*params)
    gathered = cube_gather(packed, *sizes, True, 1)
    weights = [unpack_layer(gathered[layer], depth) for layer in range(layers)]
    saved_all = []
    for layer in range(layers):
        residual, saved = layer_forward(residual, weights[layer], sizes, layer)
        saved_all.append(saved)
    encoded = residual.astype(jnp.bfloat16).reshape(groups, frame_count, width)
    upstream = out_grad.astype(jnp.float32).reshape(groups * frame_count, width)
    shards = [None] * layers
    for layer in reversed(range(layers)):
        upstream, grad_terms = layer_backward(
            upstream, saved_all[layer], weights[layer], sizes, layer
        )
        terms = pack_grads(grad_terms, count, packed.shape[1])
        shards[layer] = unpack_shard(cube_scatter(terms, *sizes, True, 6 + layer), depth)
    outputs = tuple(jnp.stack(pieces) for pieces in zip(*shards))
    return (encoded, upstream.reshape(groups, frame_count, width)) + outputs


def solution(mesh):
    sizes = (mesh.shape["clip"], mesh.shape["seq"])
    specs = (
        P("clip", "seq", None),
        P("clip", "seq", None),
        P(None, ("clip", "seq"), None),
        P(None, ("clip", "seq"), None),
        P(None, ("clip", "seq"), None),
        P(None, ("clip", "seq"), None),
        P(None, None, ("clip", "seq")),
        P(None, None, ("clip", "seq")),
        P(None, ("clip", "seq")),
    )
    return jax.shard_map(
        functools.partial(body, sizes), mesh=mesh, in_specs=specs, out_specs=specs, check_vma=False
    )
```

```python
import functools

import jax
import jax.numpy as jnp
from jax import lax
from jax.experimental import pallas as pl
from jax.experimental.pallas import tpu as pltpu
from jax.sharding import PartitionSpec as P

D = 768
H = 12
HD = 64


eps_norm = 1e-05
root_half = 0.7071067811865476
inv_root_two_pi = 0.3989422804014327


def product(left, right):
    return jnp.dot(left, right, preferred_element_type=jnp.float32)


def product_left(left, right):
    return lax.dot_general(
        left, right, (((0,), (0,)), ((), ())), preferred_element_type=jnp.float32
    )


def product_right(left, right):
    return lax.dot_general(
        left, right, (((1,), (1,)), ((), ())), preferred_element_type=jnp.float32
    )


def norm_forward(rows, gain, shift):
    center = rows - jnp.mean(rows, axis=1, keepdims=True)
    inv_scale = lax.rsqrt(jnp.mean(center * center, axis=1, keepdims=True) + eps_norm)
    unit_rows = center * inv_scale
    return (unit_rows * gain + shift, unit_rows, inv_scale)


def norm_backward(upstream, unit_rows, inv_scale, gain):
    scaled = upstream * gain
    mean_plain = jnp.mean(scaled, axis=1, keepdims=True)
    mean_unit = jnp.mean(scaled * unit_rows, axis=1, keepdims=True)
    back = inv_scale * (scaled - mean_plain - unit_rows * mean_unit)
    return (back, jnp.sum(upstream * unit_rows, axis=0), jnp.sum(upstream, axis=0))


def gelu_slope(pre_gelu):
    cumulative = 0.5 * (1.0 + lax.erf(pre_gelu * root_half))
    density = jnp.exp(-0.5 * pre_gelu * pre_gelu) * inv_root_two_pi
    return cumulative + pre_gelu * density


def column_sums(rows):
    return jnp.sum(rows.astype(jnp.float32), axis=0)


def bit_of(index, weight):
    return lax.rem(lax.div(index, weight), 2)


def flip(index, weight):
    return index + weight - 2 * weight * bit_of(index, weight)


def bit_orders(clip_size, seq_size, with_clip=True):
    high = []
    weight = clip_size * seq_size // 2
    while weight >= seq_size and with_clip:
        high.append(weight)
        weight //= 2
    low = []
    weight = seq_size // 2
    while weight >= 1:
        low.append(weight)
        weight //= 2
    first = high + low
    if not high:
        return (first, first)
    second = high[:-1] + [low[0], high[-1]] + low[1:]
    return (first, second)


def spread(position, weights):
    total = 0
    for place, weight in enumerate(weights):
        total = total + weight * lax.rem(lax.div(position, 2**place), 2)
    return total


def partner_id(weight, seq_size):
    clip_at, seq_at = lax.axis_index("clip"), lax.axis_index("seq")
    if weight < seq_size:
        return {"clip": clip_at, "seq": flip(seq_at, weight)}
    return {"clip": flip(clip_at, weight // seq_size), "seq": seq_at}


def greet(weights, seq_size):
    barrier = pltpu.get_barrier_semaphore()
    for weight in weights:
        pl.semaphore_signal(
            barrier,
            inc=1,
            device_id=partner_id(weight, seq_size),
            device_id_type=pl.DeviceIdType.MESH,
        )
    pl.semaphore_wait(barrier, len(weights))


def round_up(value, step):
    return (value + step - 1) // step * step


def own_index(seq_size, with_clip):
    seq_at = lax.axis_index("seq")
    return lax.axis_index("clip") * seq_size + seq_at if with_clip else seq_at


def cube_gather(arrays, pieces, chains, sizes, with_clip, collective_id):
    clip_size, seq_size = sizes
    count = clip_size * seq_size if with_clip else seq_size
    orders = bit_orders(clip_size, seq_size, with_clip)
    stages = len(orders[0])
    last = max(chain[2] for chain in chains)

    def kernel(*refs):
        in_refs = refs[: len(arrays)]
        out_refs = refs[len(arrays) : len(arrays) + len(pieces)]
        own_sem, send_sem, recv_sem = refs[len(arrays) + len(pieces) :]
        greet(orders[0], seq_size)
        me = own_index(seq_size, with_clip)
        own = []
        for at, (array_at, index, _, _) in enumerate(pieces):
            copy = pltpu.make_async_copy(
                in_refs[array_at].at[index], out_refs[at].at[me], own_sem.at[at]
            )
            copy.start()
            own.append(copy)
        for copy in own:
            copy.wait()

        def transfer(at, stage, weight, source):
            return pltpu.make_async_remote_copy(
                src_ref=source,
                dst_ref=source,
                send_sem=send_sem.at[at, stage],
                recv_sem=recv_sem.at[at, stage],
                device_id=partner_id(weight, seq_size),
                device_id_type=pl.DeviceIdType.MESH,
            )

        def start_stage(chain, stage):
            order = orders[chain[1]]
            base = me
            for done in order[:stage]:
                base = base - done * bit_of(me, done)

            def one(position, carry):
                place = base + spread(position, order[:stage])
                for at in chain[0]:
                    transfer(at, stage, order[stage], out_refs[at].at[place]).start()
                return carry

            if stage == 0:
                one(0, 0)
            else:
                lax.fori_loop(0, 2**stage, one, 0)

        def wait_stage(chain, stage):
            for at in chain[0]:
                block = out_refs[at].at[pl.ds(0, 2**stage)]
                transfer(at, stage, orders[chain[1]][stage], block).wait()

        for tick in range(stages + last + 1):
            for chain in chains:
                stage = tick - chain[2]
                if 1 <= stage <= stages:
                    wait_stage(chain, stage - 1)
                if 0 <= stage < stages:
                    start_stage(chain, stage)

    return pl.pallas_call(
        kernel,
        out_shape=tuple(
            jax.ShapeDtypeStruct((count, rows, columns), jnp.bfloat16)
            for _, _, rows, columns in pieces
        ),
        in_specs=[pl.BlockSpec(memory_space=pl.ANY)] * len(arrays),
        out_specs=(pl.BlockSpec(memory_space=pl.ANY),) * len(pieces),
        scratch_shapes=[
            pltpu.SemaphoreType.DMA((len(pieces),)),
            pltpu.SemaphoreType.DMA((len(pieces), stages)),
            pltpu.SemaphoreType.DMA((len(pieces), stages)),
        ],
        compiler_params=pltpu.CompilerParams(
            collective_id=collective_id, has_side_effects=True, vmem_limit_bytes=16 * 2**20
        ),
    )(*arrays)


def cube_scatter(terms, chains, sizes, with_clip, collective_id, out_dtype):
    clip_size, seq_size = sizes
    count = terms[0].shape[0]
    orders = [order[::-1] for order in bit_orders(clip_size, seq_size, with_clip)]
    stages = len(orders[0])
    offsets = [sum(count // 2 ** (s + 1) for s in range(stage)) for stage in range(stages)]
    last = max(chain[2] for chain in chains)
    number = len(terms)

    def kernel(*refs):
        in_refs, out_refs = refs[:number], refs[number : 2 * number]
        totals, landeds = refs[2 * number : 3 * number], refs[3 * number : 4 * number]
        own_sem, send_sem, recv_sem = refs[4 * number :]
        greet(orders[0], seq_size)
        me = own_index(seq_size, with_clip)

        def transfer(at, stage, order, source, target):
            return pltpu.make_async_remote_copy(
                src_ref=source,
                dst_ref=target,
                send_sem=send_sem.at[at, stage],
                recv_sem=recv_sem.at[at, stage],
                device_id=partner_id(order[stage], seq_size),
                device_id_type=pl.DeviceIdType.MESH,
            )

        def first_place(order, position, mine):
            weight = order[0]
            bit = bit_of(me, weight) if mine else 1 - bit_of(me, weight)
            return weight * bit + spread(position, order[:0:-1])

        def bases(order, stage):
            base = 0
            for at in range(1, stage):
                base = base + count // 2 ** (at + 1) * bit_of(me, order[at])
            step = count // 2 ** (stage + 1)
            bit = bit_of(me, order[stage])
            return base + step * bit, base + step * (1 - bit)

        def start_stage(chain, stage):
            order = orders[chain[1]]
            blocks = count // 2 ** (stage + 1)
            if stage == 0:

                def one(position, carry):
                    for at in chain[0]:
                        source = in_refs[at].at[first_place(order, position, False)]
                        transfer(at, 0, order, source, landeds[at].at[position]).start()
                    return carry

                def load(position, carry):
                    for at in chain[0]:
                        source = in_refs[at].at[first_place(order, position, True)]
                        pltpu.make_async_copy(
                            source, totals[at].at[position], own_sem.at[at]
                        ).start()
                    return carry

                lax.fori_loop(0, blocks, one, 0)
                lax.fori_loop(0, blocks, load, 0)
            else:
                theirs = bases(order, stage)[1]
                for at in chain[0]:
                    source = totals[at].at[pl.ds(theirs, blocks)]
                    target = landeds[at].at[pl.ds(offsets[stage], blocks)]
                    transfer(at, stage, order, source, target).start()

        def finish_stage(chain, stage):
            order = orders[chain[1]]
            blocks = count // 2 ** (stage + 1)
            mine = bases(order, stage)[0] if stage else 0
            for at in chain[0]:
                source = (totals[at] if stage else in_refs[at]).at[pl.ds(0, blocks)]
                target = landeds[at].at[pl.ds(offsets[stage], blocks)]
                transfer(at, stage, order, source, target).wait()
                if stage == 0:
                    pltpu.make_async_copy(source, totals[at], own_sem.at[at]).wait()
                rows, columns = terms[at].shape[1:]
                high = rows if rows % 32 else 32
                tiles, wide = rows // high, D

                def add(step, carry, at=at, tiles=tiles, high=high, wide=wide, columns=columns):
                    position, tile = lax.div(step, tiles), lax.rem(step, tiles)
                    row = pl.ds(0, high)
                    if tiles > 1:
                        row = pl.ds(pl.multiple_of(tile * high, high), high)
                    for start in range(0, columns, wide):
                        part = pl.ds(start, wide)
                        summed = totals[at][mine + position, row, part].astype(
                            jnp.float32
                        ) + landeds[at][offsets[stage] + position, row, part].astype(jnp.float32)
                        if stage == stages - 1:
                            out_refs[at][row, part] = summed.astype(out_dtype)
                        else:
                            totals[at][mine + position, row, part] = summed.astype(jnp.bfloat16)
                    return carry

                lax.fori_loop(0, blocks * tiles, add, 0)

        for tick in range(stages + last + 1):
            for chain in chains:
                stage = tick - chain[2]
                if 1 <= stage <= stages:
                    finish_stage(chain, stage - 1)
                if 0 <= stage < stages:
                    start_stage(chain, stage)

    return pl.pallas_call(
        kernel,
        out_shape=tuple(jax.ShapeDtypeStruct(term.shape[1:], out_dtype) for term in terms),
        in_specs=[pl.BlockSpec(memory_space=pl.ANY)] * number,
        out_specs=(pl.BlockSpec(memory_space=pltpu.VMEM),) * number,
        scratch_shapes=[pltpu.VMEM((count // 2,) + t.shape[1:], t.dtype) for t in terms]
        + [pltpu.VMEM((count - 1,) + t.shape[1:], t.dtype) for t in terms]
        + [
            pltpu.SemaphoreType.DMA((number,)),
            pltpu.SemaphoreType.DMA((number, stages)),
            pltpu.SemaphoreType.DMA((number, stages)),
        ],
        compiler_params=pltpu.CompilerParams(
            collective_id=collective_id, has_side_effects=True, vmem_limit_bytes=56 * 2**20
        ),
    )(*terms)


def head_pair(ref, head):
    return ref[:, head * HD : (head + 1) * HD]


def probabilities(query, key):
    scores = product_right(query, key) * (HD ** (-0.5))
    powers = jnp.exp(scores - jnp.max(scores, axis=1, keepdims=True))
    return powers * (1.0 / jnp.sum(powers, axis=1, keepdims=True))


def attend_forward_kernel(q_ref, k_ref, v_ref, o_ref):
    outputs = []
    for head in range(2):
        probs = probabilities(head_pair(q_ref, head), head_pair(k_ref, head))
        outputs.append(product(probs.astype(jnp.bfloat16), head_pair(v_ref, head)))
    o_ref[...] = jnp.concatenate(outputs, axis=1).astype(o_ref.dtype)


def attend_backward_kernel(q_ref, k_ref, v_ref, go_ref, gq_ref, gk_ref, gv_ref):
    grads = ([], [], [])
    for head in range(2):
        query, key = head_pair(q_ref, head), head_pair(k_ref, head)
        value, upstream = head_pair(v_ref, head), head_pair(go_ref, head)
        probs = probabilities(query, key)
        grad_probs = product_right(upstream, value)
        inner = jnp.sum(grad_probs * probs, axis=1, keepdims=True)
        grad_scores = (probs * (grad_probs - inner)).astype(jnp.bfloat16)
        grads[0].append(product(grad_scores, key) * (HD ** (-0.5)))
        grads[1].append(product_left(grad_scores, query) * (HD ** (-0.5)))
        grads[2].append(product_left(probs.astype(jnp.bfloat16), upstream))
    for ref, pieces in zip((gq_ref, gk_ref, gv_ref), grads):
        ref[...] = jnp.concatenate(pieces, axis=1).astype(ref.dtype)


def attend_forward(projected, keys, values):
    rows, length = projected.shape[0], keys.shape[0]
    pairs = D // (2 * HD)
    return pl.pallas_call(
        attend_forward_kernel,
        grid=(pairs,),
        out_shape=jax.ShapeDtypeStruct((rows, D), jnp.bfloat16),
        in_specs=[
            pl.BlockSpec((rows, 2 * HD), lambda pair: (0, pair)),
            pl.BlockSpec((length, 2 * HD), lambda pair: (0, pair)),
            pl.BlockSpec((length, 2 * HD), lambda pair: (0, pair)),
        ],
        out_specs=pl.BlockSpec((rows, 2 * HD), lambda pair: (0, pair)),
        compiler_params=pltpu.CompilerParams(vmem_limit_bytes=40 * 2**20),
    )(projected, keys, values)


def attend_backward(projected, keys, values, grad_attended):
    rows, length = projected.shape[0], keys.shape[0]
    pairs = D // (2 * HD)
    return pl.pallas_call(
        attend_backward_kernel,
        grid=(pairs,),
        out_shape=(
            jax.ShapeDtypeStruct((rows, D), jnp.bfloat16),
            jax.ShapeDtypeStruct((length, D), jnp.bfloat16),
            jax.ShapeDtypeStruct((length, D), jnp.bfloat16),
        ),
        in_specs=[
            pl.BlockSpec((rows, 2 * HD), lambda pair: (0, pair)),
            pl.BlockSpec((length, 2 * HD), lambda pair: (0, pair)),
            pl.BlockSpec((length, 2 * HD), lambda pair: (0, pair)),
            pl.BlockSpec((rows, 2 * HD), lambda pair: (0, pair)),
        ],
        out_specs=(
            pl.BlockSpec((rows, 2 * HD), lambda pair: (0, pair)),
            pl.BlockSpec((length, 2 * HD), lambda pair: (0, pair)),
            pl.BlockSpec((length, 2 * HD), lambda pair: (0, pair)),
        ),
        compiler_params=pltpu.CompilerParams(vmem_limit_bytes=48 * 2**20),
    )(projected, keys, values, grad_attended)


def small_pad(small):
    rows = round_up((small.shape[-1] + D - 1) // D, 16)
    padding = [(0, 0)] * (small.ndim - 1) + [(0, rows * D - small.shape[-1])]
    return jnp.pad(small, padding).reshape(small.shape[:-1] + (rows, D))


def pack_small(norm_gains, shifts, mlp_bias):
    layers = norm_gains.shape[0]
    return small_pad(
        jnp.concatenate(
            [norm_gains.reshape(layers, -1), shifts.reshape(layers, -1), mlp_bias], axis=1
        )
    )


def unpack_layer(gathered, depth):
    count = gathered[0].shape[0]
    matrices = tuple(piece.reshape(-1, piece.shape[2]) for piece in gathered[:4])
    small = gathered[4].reshape(count, -1)[:, : 12 * depth].astype(jnp.float32)
    gains = small[:, : 2 * depth].reshape(count, 2, depth).transpose(1, 0, 2).reshape(2, D)
    shift_rows = small[:, 2 * depth : 8 * depth].reshape(count, 6, depth)
    shift_rows = shift_rows.transpose(1, 0, 2).reshape(6, D)
    bias_mlp = small[:, 8 * depth :].reshape(4 * D)
    return matrices + (gains, shift_rows, bias_mlp)


def by_owner(grad_terms, count):
    gains, shift_rows, bias = grad_terms[4:]
    depth = D // count
    small = jnp.concatenate(
        [
            gains.reshape(2, count, depth).transpose(1, 0, 2).reshape(count, -1),
            shift_rows.reshape(6, count, depth).transpose(1, 0, 2).reshape(count, -1),
            bias.reshape(count, -1),
        ],
        axis=1,
    ).astype(jnp.bfloat16)
    matrices = [
        term.astype(jnp.bfloat16).reshape(count, -1, term.shape[1]) for term in grad_terms[:4]
    ]
    return matrices + [small_pad(small)]


def unpack_shard(summed, depth):
    small = summed[4].reshape(-1)
    return tuple(summed[:4]) + (
        small[: 2 * depth].reshape(2, depth),
        small[2 * depth : 8 * depth].reshape(6, depth),
        small[8 * depth : 12 * depth],
    )


def layer_chains(layers):
    chains = []
    for place, layer in enumerate(layers):
        chains.append(([5 * layer, 5 * layer + 3], 0, place))
        chains.append(([5 * layer + 1, 5 * layer + 2, 5 * layer + 4], 1, place))
    return chains


def layer_forward(residual, weights, sizes, layer_index):
    w_attn_in, w_attn_out, w_mlp_in, w_mlp_out, gain_rows, shift_rows, bias_mlp = weights
    normed = norm_forward(residual, gain_rows[0], shift_rows[0])[0].astype(jnp.bfloat16)
    qkv_bias = jnp.concatenate([shift_rows[1], jnp.zeros_like(shift_rows[1]), shift_rows[2]])
    projected = (product(normed, w_attn_in) + qkv_bias).astype(jnp.bfloat16)
    rows = projected.shape[0]
    keys, values = cube_gather(
        (projected,),
        [(0, (slice(None), pl.ds(D * at, D)), rows, D) for at in (1, 2)],
        [([0], 0, 0), ([1], 0, 0)],
        sizes,
        False,
        2 + layer_index,
    )
    keys, values = keys.reshape(-1, D), values.reshape(-1, D)
    attended = attend_forward(projected, keys, values)
    middle = residual + product(attended, w_attn_out) + shift_rows[3]
    normed_two = norm_forward(middle, gain_rows[1], shift_rows[4])[0].astype(jnp.bfloat16)
    pre_gelu = product(normed_two, w_mlp_in) + bias_mlp
    hidden = jax.nn.gelu(pre_gelu, approximate=False).astype(jnp.bfloat16)
    result = middle + product(hidden, w_mlp_out) + shift_rows[5]
    saved = (residual, normed, projected, keys, values, attended, middle, normed_two, pre_gelu, hidden)
    return (result, saved)


def layer_backward(upstream, saved, weights, sizes, layer_index):
    w_attn_in, w_attn_out, w_mlp_in, w_mlp_out, gain_rows, shift_rows, bias_mlp = weights
    residual, normed, projected, keys, values, attended, middle, normed_two, pre_gelu, hidden = saved
    upstream_low = upstream.astype(jnp.bfloat16)
    grad_mlp_out = product_left(hidden, upstream_low)
    grad_bias_two = column_sums(upstream_low)
    grad_pre = (product_right(upstream_low, w_mlp_out) * gelu_slope(pre_gelu)).astype(jnp.bfloat16)
    grad_mlp_in = product_left(normed_two, grad_pre)
    grad_mlp_bias = column_sums(grad_pre)
    grad_normed_two = product_right(grad_pre, w_mlp_in)
    unit_two, scale_two = norm_forward(middle, gain_rows[1], shift_rows[4])[1:]
    back_two, grad_gain_two, grad_shift_two = norm_backward(
        grad_normed_two, unit_two, scale_two, gain_rows[1]
    )
    grad_middle = upstream + back_two
    middle_low = grad_middle.astype(jnp.bfloat16)
    grad_attn_out = product_left(attended, middle_low)
    grad_bias_out = column_sums(middle_low)
    grad_attended = product_right(middle_low, w_attn_out).astype(jnp.bfloat16)
    grad_queries, key_terms, value_terms = attend_backward(projected, keys, values, grad_attended)
    rows = grad_queries.shape[0]
    grad_keys, grad_values = cube_scatter(
        (key_terms.reshape(-1, rows, D), value_terms.reshape(-1, rows, D)),
        [([0], 0, 0), ([1], 0, 0)],
        sizes,
        False,
        4 + layer_index,
        jnp.bfloat16,
    )
    grad_projected = jnp.concatenate([grad_queries, grad_keys, grad_values], axis=1)
    grad_attn_in = product_left(normed, grad_projected)
    projected_sums = column_sums(grad_projected)
    grad_normed = product_right(grad_projected, w_attn_in)
    unit_one, scale_one = norm_forward(residual, gain_rows[0], shift_rows[0])[1:]
    back_one, grad_gain_one, grad_shift_one = norm_backward(
        grad_normed, unit_one, scale_one, gain_rows[0]
    )
    grad_residual = grad_middle + back_one
    grad_gains = jnp.stack([grad_gain_one, grad_gain_two])
    grad_shifts = jnp.stack(
        [
            grad_shift_one,
            projected_sums[:D],
            projected_sums[2 * D :],
            grad_bias_out,
            grad_shift_two,
            grad_bias_two,
        ]
    )
    grad_terms = (
        grad_attn_in,
        grad_attn_out,
        grad_mlp_in,
        grad_mlp_out,
        grad_gains,
        grad_shifts,
        grad_mlp_bias,
    )
    return (grad_residual, grad_terms)


def body(sizes, frames, out_grad, *params):
    layers, depth = params[0].shape[0], params[0].shape[1]
    count = sizes[0] * sizes[1]
    groups, frame_count, width = frames.shape
    residual = frames.astype(jnp.float32).reshape(groups * frame_count, width)
    arrays = tuple(params[:4]) + (pack_small(*params[4:]),)
    pieces = [
        (at, layer) + array.shape[1:] for layer in range(layers) for at, array in enumerate(arrays)
    ]
    gathered = cube_gather(arrays, pieces, layer_chains(range(layers)), sizes, True, 1)
    weights = [
        unpack_layer(gathered[5 * layer : 5 * layer + 5], depth) for layer in range(layers)
    ]
    saved_all = []
    for layer in range(layers):
        residual, saved = layer_forward(residual, weights[layer], sizes, layer)
        saved_all.append(saved)
    encoded = residual.astype(jnp.bfloat16).reshape(groups, frame_count, width)
    upstream = out_grad.astype(jnp.float32).reshape(groups * frame_count, width)
    terms = [None] * layers
    for layer in reversed(range(layers)):
        upstream, grad_terms = layer_backward(
            upstream, saved_all[layer], weights[layer], sizes, layer
        )
        terms[layer] = by_owner(grad_terms, count)
    if depth % 8 == 0:
        summed = cube_scatter(
            sum(terms, []), layer_chains(range(layers)), sizes, True, 6, jnp.float32
        )
    else:
        summed = ()
        for layer in range(layers):
            summed += tuple(
                cube_scatter(terms[layer], layer_chains([0]), sizes, True, 6 + layer, jnp.float32)
            )
    shards = [unpack_shard(summed[5 * layer : 5 * layer + 5], depth) for layer in range(layers)]
    outputs = tuple(jnp.stack(pieces) for pieces in zip(*shards))
    return (encoded, upstream.reshape(groups, frame_count, width)) + outputs


def solution(mesh):
    sizes = (mesh.shape["clip"], mesh.shape["seq"])
    specs = (
        P("clip", "seq", None),
        P("clip", "seq", None),
        P(None, ("clip", "seq"), None),
        P(None, ("clip", "seq"), None),
        P(None, ("clip", "seq"), None),
        P(None, ("clip", "seq"), None),
        P(None, None, ("clip", "seq")),
        P(None, None, ("clip", "seq")),
        P(None, ("clip", "seq")),
    )
    return jax.shard_map(
        functools.partial(body, sizes), mesh=mesh, in_specs=specs, out_specs=specs, check_vma=False
    )
```
